256 devices in a mesh: hst: 32 (over y, x, core), tensor: 8 (over z).
Axes of the slice: x: 4, y: 4, z: 8, core: 2. Of those that a mesh axis runs over, the one named last changes fastest.
Arguments:
- queries: bfloat16 [16384, 8192], P('hst', 'tensor'), may hold values from -220 to 220
- own_kv: bfloat16 [16384, 2048], P('hst', 'tensor'), may hold values from -6 to 6
- retain: int32 [2048, 8], P('hst', 'tensor'), may hold values from 0 to 511, as said below
- anchor_hidden: bfloat16 [1024, 8192], P(('hst', 'tensor')), may hold values from -6 to 6
- w_kv: bfloat16 [8192, 2048], P(None, 'tensor'), may hold values from -0.0625 to 0.0625
Outputs:
- attended: bfloat16 [16384, 8192], P('hst', 'tensor')
The draws below stay inside these ranges and needn't reach their ends.
Inputs may be any that keep to these rules, and one draw needn't show every extreme that they name: `retain`: each host block and key-value head names 64 distinct local rows, 0 and 511 among them.
All inputs are finite; a program needn't handle non-finite values.
Results may differ from the reference program's by a relative error of at most 0.023.
Values may be sent and summed in bfloat16 or wider, within the bound.
No kernel may reach another device: no remote copies, remote signals or barrier semaphores. Data moves between devices by JAX's collectives and lax.ppermute only.
A program may use at most 128 MiB of HBM per device.

```python
import jax
import jax.numpy as jnp
from jax import lax

D = 8192
H = 64
KVH = 8
HD = 128
TOK_DEV = 512
ANCHOR = 1024
RET = 64
TOKENS = 16384
N_HST = 32


def draw_queries(key, part):
    key = jax.random.fold_in(key, 2)
    first = jax.random.fold_in(key, 11)
    base = jnp.clip(jax.random.normal(first, (TOKENS, H * HD), jnp.float32), -6.0, 6.0)
    return base.astype(jnp.bfloat16)


def draw_retain(key, part):
    key = jax.random.fold_in(key, 1)

    def one_list(number):
        pick_key = jax.random.fold_in(key, 2 * number)
        order_key = jax.random.fold_in(key, 2 * number + 1)
        picked = jax.random.permutation(pick_key, TOK_DEV - 2)[:RET - 2] + 1
        listed = jnp.concatenate([jnp.array([0, TOK_DEV - 1], jnp.int32), picked.astype(jnp.int32)])
        return jax.random.permutation(order_key, listed)
    lists = jax.vmap(one_list)(jnp.arange(N_HST * KVH, dtype=jnp.int32))
    lists = lists.reshape(N_HST, KVH, RET)
    return jnp.transpose(lists, (0, 2, 1)).reshape(N_HST * RET, KVH).astype(jnp.int32)


def block_levels(key, extent, pieces, least, high):
    gain, own = 1.0, jax.random.fold_in(key, 6)
    for axis_at, blocks in pieces:
        draws = jnp.exp(jax.random.uniform(jax.random.fold_in(own, axis_at), (blocks,), jnp.float32, least / len(pieces), high / len(pieces)))
        gain = gain * jnp.repeat(draws, extent[axis_at] // blocks).reshape([-1 if axis == axis_at else 1 for axis in range(len(extent))])
    return gain


def normal_values(own_key, dims, width, most, shards=(), kind=jnp.bfloat16):
    gain = block_levels(own_key, dims, shards, -0.22, 0.18) if shards else 1.0
    drawn = jax.random.normal(own_key, dims, jnp.float32) * width * gain
    return jnp.minimum(jnp.maximum(drawn, -most), most).astype(kind)


def setup_inputs(seed: int = 0) -> dict:
    streams_of = jax.random.split(jax.random.key(seed), 6)
    queries = draw_queries(jax.random.fold_in(streams_of[5], 71), 0)
    own_kv = normal_values(streams_of[1], (TOKENS, KVH * 2 * HD), 1.0, 6.0, ((0, 32), (1, 8)))
    retain = draw_retain(jax.random.fold_in(streams_of[5], 71), 0)
    anchor_hidden = normal_values(streams_of[3], (ANCHOR, D), 1.0, 6.0, ((0, 256),))
    w_kv = normal_values(streams_of[4], (D, KVH * 2 * HD), D ** -0.5, 0.0625, ((1, 8),))
    return dict(queries=queries, own_kv=own_kv, retain=retain, anchor_hidden=anchor_hidden, w_kv=w_kv)


def reference(queries, own_kv, retain, anchor_hidden, w_kv):
    group = H // KVH
    scale = 1.0 / (HD ** 0.5)
    anchor_kv = jnp.dot(anchor_hidden, w_kv, preferred_element_type=jnp.float32).astype(jnp.bfloat16)
    anchor = anchor_kv.reshape(ANCHOR, KVH, 2 * HD)
    blocks = own_kv.reshape(N_HST, TOK_DEV, KVH, 2 * HD)
    index = retain.reshape(N_HST, RET, KVH).astype(jnp.int32)
    kept = jnp.take_along_axis(blocks, index[..., None], axis=1).reshape(N_HST * RET, KVH, 2 * HD)
    query_blocks = queries.reshape(N_HST, TOK_DEV, KVH, group, HD)
    kept_host = jnp.arange(N_HST * RET, dtype=jnp.int32) // RET
    rows = jnp.arange(TOK_DEV, dtype=jnp.int32)

    def one_host(items):
        query_host, own_host, host = items
        seen = jnp.concatenate([jnp.ones((TOK_DEV, ANCHOR), bool),
                                jnp.broadcast_to((kept_host < host)[None, :], (TOK_DEV, N_HST * RET)),
                                rows[None, :] <= rows[:, None]], axis=1)

        def one_head(head_items):
            query_head, anchor_head, kept_head, own_head = head_items
            keys_all = jnp.concatenate([anchor_head, kept_head, own_head], axis=0).astype(jnp.float32)
            scores = jnp.einsum('tqd,ld->qtl', query_head.astype(jnp.float32), keys_all[:, :HD]) * scale
            scores = jnp.where(seen[None], scores, -1e30)
            top = jnp.max(scores, axis=-1, keepdims=True)
            weights = jnp.where(seen[None], jnp.exp(scores - top), 0.0)
            total = jnp.sum(weights, axis=-1)
            summed = jnp.einsum('qtl,ld->tqd', weights.astype(jnp.bfloat16).astype(jnp.float32), keys_all[:, HD:])
            return (summed / jnp.transpose(total)[:, :, None]).astype(jnp.bfloat16)

        heads = lax.map(one_head, (jnp.moveaxis(query_host, 1, 0), jnp.moveaxis(anchor, 1, 0),
                                   jnp.moveaxis(kept, 1, 0), jnp.moveaxis(own_host, 1, 0)))
        return jnp.moveaxis(heads, 0, 1)

    result = lax.map(one_host, (query_blocks, blocks, jnp.arange(N_HST, dtype=jnp.int32)))
    return result.reshape(TOKENS, H * HD)
```

```python
import functools

import jax
import jax.numpy as jnp
from jax import lax
from jax.experimental import pallas as pl
from jax.experimental.pallas import tpu as pltpu
from jax.sharding import PartitionSpec as P

H = 64
KVH = 8
HD = 128
GROUP = H // KVH
EXP2_SCALE = 1.4426950408889634 / HD**0.5
AUG = HD + 16
KEY_BLOCK = 256
KEPT_BLOCK = 512
SAFE_TOTAL = 2.0**100


def mul_nt(a, b):
    return lax.dot_general(a, b, (((1,), (1,)), ((), ())), preferred_element_type=jnp.float32)


def mul(a, b):
    return lax.dot_general(a, b, (((1,), (0,)), ((), ())), preferred_element_type=jnp.float32)


def weights_of(scores, top):
    return jnp.exp2((scores - top) * EXP2_SCALE).astype(jnp.bfloat16)


def head_cols(head):
    return pl.ds(pl.multiple_of(head * HD, HD), HD)


def fill_values(vt_ref, kv_ref):
    vt_ref[:HD, :] = kv_ref[:, HD:].T
    vt_ref[HD:, :] = jnp.ones((AUG - HD, vt_ref.shape[1]), jnp.bfloat16)


def select_kernel(retain_ref, own_ref, out_ref):
    tok = own_ref.shape[0]
    picks = retain_ref[...] == lax.broadcasted_iota(jnp.int32, (retain_ref.shape[0], tok), 1)
    kept = mul(jnp.where(picks, 1.0, 0.0).astype(jnp.bfloat16), own_ref[...]).astype(jnp.bfloat16)
    for copy in range(out_ref.shape[0]):
        out_ref[copy] = kept


def project_kernel(rows_ref, w_ref, out_ref):
    rows = jnp.concatenate([rows_ref[i] for i in range(rows_ref.shape[0])], axis=0)
    part = mul(rows, w_ref[...]).astype(jnp.bfloat16)
    for copy in range(out_ref.shape[0]):
        out_ref[copy] = part


def own_kernel(q_ref, kv_ref, top_ref, acc_ref, vt_ref):
    tok = q_ref.shape[0]
    fill_values(vt_ref, kv_ref)
    keys = lax.broadcasted_iota(jnp.int32, (KEY_BLOCK, KEY_BLOCK), 0)
    queries = lax.broadcasted_iota(jnp.int32, (KEY_BLOCK, KEY_BLOCK), 1)
    seen = keys <= queries

    def one_head(head):
        for block in range(tok // KEY_BLOCK):
            at = slice(block * KEY_BLOCK, (block + 1) * KEY_BLOCK)
            q = q_ref[at, head_cols(head)]
            parts = [
                mul_nt(kv_ref[i * KEY_BLOCK : (i + 1) * KEY_BLOCK, :HD], q) for i in range(block + 1)
            ]
            parts[-1] = jnp.where(seen, parts[-1], -1e30)
            top = functools.reduce(
                jnp.maximum, [jnp.max(part, axis=0, keepdims=True) for part in parts]
            )
            acc = None
            for i, part in enumerate(parts):
                term = mul(vt_ref[:, i * KEY_BLOCK : (i + 1) * KEY_BLOCK], weights_of(part, top))
                acc = term if acc is None else acc + term
            top_ref[pl.ds(head, 1), at] = top
            acc_ref[pl.ds(head, 1), :, at] = acc[None]

    def step(i, carry):
        one_head(2 * i)
        one_head(2 * i + 1)
        return carry

    lax.fori_loop(0, GROUP // 2, step, 0)


def careful_block(q, keys, values, valid, top, acc):
    scores = mul_nt(keys, q)
    if valid is not None:
        scores = jnp.where(valid, scores, -1e30)
    new_top = jnp.maximum(top, jnp.max(scores, axis=0, keepdims=True))
    weights = weights_of(scores, new_top)
    return new_top, acc * jnp.exp2((top - new_top) * EXP2_SCALE) + mul(values, weights)


def kept_kernel(count_ref, q_ref, kv_ref, top_ref, acc_ref, new_top_ref, new_acc_ref, vt_ref):
    count = count_ref[0]
    blocks = lax.div(count + KEPT_BLOCK - 1, KEPT_BLOCK)
    fill_values(vt_ref, kv_ref)
    spare = lax.broadcasted_iota(jnp.int32, vt_ref.shape, 1) >= count
    vt_ref[...] = jnp.where(spare, 0.0, vt_ref[...]).astype(jnp.bfloat16)
    new_top_ref[...] = top_ref[...]
    new_acc_ref[...] = acc_ref[...]

    def one_head(head, first):
        q = q_ref[:, head_cols(head)]
        top = top_ref[pl.ds(head, 1), :]
        acc = new_acc_ref[head]
        for i in range(KEPT_BLOCK // KEY_BLOCK):
            at = pl.ds(pl.multiple_of(first + i * KEY_BLOCK, KEY_BLOCK), KEY_BLOCK)
            weights = weights_of(mul_nt(kv_ref[at, :HD], q), top)
            acc = acc + mul(vt_ref[:, at], weights)
        new_acc_ref[head] = acc

    def step(i, carry):
        first = lax.div(i, GROUP // 2) * KEPT_BLOCK
        head = lax.rem(i, GROUP // 2) * 2
        one_head(head, first)
        one_head(head + 1, first)
        return carry

    lax.fori_loop(0, blocks * (GROUP // 2), step, 0)
    totals = new_acc_ref[:, HD : HD + 8, :]
    safe = jnp.all(totals < SAFE_TOTAL)

    @pl.when(jnp.logical_not(safe))
    def careful():
        def head_step(head, carry):
            q = q_ref[:, head_cols(head)]
            new_top_ref[pl.ds(head, 1), :] = top_ref[pl.ds(head, 1), :]
            new_acc_ref[head] = acc_ref[head]

            def block_step(block, carry):
                at = pl.ds(pl.multiple_of(block * KEY_BLOCK, KEY_BLOCK), KEY_BLOCK)
                valid = (
                    lax.broadcasted_iota(jnp.int32, (KEY_BLOCK, 1), 0) + block * KEY_BLOCK < count
                )
                top, acc = careful_block(
                    q,
                    kv_ref[at, :HD],
                    vt_ref[:, at],
                    valid,
                    new_top_ref[pl.ds(head, 1), :],
                    new_acc_ref[head],
                )
                new_top_ref[pl.ds(head, 1), :] = top
                new_acc_ref[head] = acc
                return carry

            return lax.fori_loop(0, blocks * (KEPT_BLOCK // KEY_BLOCK), block_step, carry)

        lax.fori_loop(0, GROUP, head_step, 0)


def anchor_kernel(q_ref, kv_ref, top_ref, acc_ref, out_ref, vt_ref, total_ref):
    fill_values(vt_ref, kv_ref)
    steps = kv_ref.shape[0] // KEY_BLOCK

    def finish(head, acc):
        result = acc[:HD] * (1.0 / acc[HD : HD + 1])
        out_ref[:, head_cols(head)] = result.T.astype(jnp.bfloat16)

    def one_head(head):
        q = q_ref[:, head_cols(head)]
        top = top_ref[pl.ds(head, 1), :]
        acc = acc_ref[head]
        for i in range(steps):
            at = slice(i * KEY_BLOCK, (i + 1) * KEY_BLOCK)
            acc = acc + mul(vt_ref[:, at], weights_of(mul_nt(kv_ref[at, :HD], q), top))
        total_ref[pl.ds(head, 1), :] = acc[HD : HD + 1]
        finish(head, acc)

    def step(i, carry):
        one_head(2 * i)
        one_head(2 * i + 1)
        return carry

    lax.fori_loop(0, GROUP // 2, step, 0)
    safe = jnp.all(total_ref[...] < SAFE_TOTAL)

    @pl.when(jnp.logical_not(safe))
    def careful():
        def head_step(head, carry):
            q = q_ref[:, head_cols(head)]
            top, acc = top_ref[pl.ds(head, 1), :], acc_ref[head]
            for i in range(steps):
                at = slice(i * KEY_BLOCK, (i + 1) * KEY_BLOCK)
                top, acc = careful_block(q, kv_ref[at, :HD], vt_ref[:, at], None, top, acc)
            finish(head, acc)
            return carry

        lax.fori_loop(0, GROUP, head_step, 0)


VMEM = pl.BlockSpec(memory_space=pltpu.VMEM)
SMEM = pl.BlockSpec(memory_space=pltpu.SMEM)


def call(kernel, name, in_specs, outs, args, scratch=(), flops=0, nbytes=0, limit=32):
    return pl.pallas_call(
        kernel,
        in_specs=in_specs,
        out_specs=[VMEM] * len(outs),
        out_shape=[jax.ShapeDtypeStruct(shape, dtype) for shape, dtype in outs],
        scratch_shapes=list(scratch),
        compiler_params=pltpu.CompilerParams(vmem_limit_bytes=limit << 20),
        cost_estimate=pl.CostEstimate(flops=flops, bytes_accessed=nbytes, transcendentals=0),
        name=name,
    )(*args)


def per_device(queries, own_kv, retain, anchor_hidden, w_kv):
    tok, width = own_kv.shape
    hosts = lax.axis_size("hst")
    heads = lax.axis_size("tensor")
    host = lax.axis_index("hst")
    kept_rows = retain.shape[0]
    rows = anchor_hidden.shape[0]
    bf16, f32 = jnp.bfloat16, jnp.float32

    with jax.named_scope("gather_hidden"):
        hidden = jnp.broadcast_to(anchor_hidden[None], (heads, *anchor_hidden.shape))
        hidden = lax.all_to_all(hidden, "tensor", 0, 0)
    with jax.named_scope("select_kept"):
        (kept,) = call(
            select_kernel,
            "select",
            [VMEM] * 2,
            [((hosts, kept_rows, width), bf16)],
            (retain, own_kv),
            flops=2 * kept_rows * tok * width,
            nbytes=2 * hosts * kept_rows * width,
        )
        kept = lax.all_to_all(kept, "hst", 0, 0).reshape(hosts * kept_rows, width)
    with jax.named_scope("own"):
        top, acc = call(
            own_kernel,
            "own",
            [VMEM] * 2,
            [((GROUP, tok), f32), ((GROUP, AUG, tok), f32)],
            (queries, own_kv),
            [pltpu.VMEM((AUG, tok), bf16)],
            flops=4 * GROUP * tok * tok * HD,
            nbytes=4 << 20,
        )
    with jax.named_scope("project"):
        (part,) = call(
            project_kernel,
            "project",
            [VMEM] * 2,
            [((hosts, heads * rows, width), bf16)],
            (hidden, w_kv),
            flops=2 * heads * rows * w_kv.shape[0] * width,
            nbytes=5 << 20,
        )
        anchor = lax.all_to_all(part, "hst", 0, 0).reshape(hosts * heads * rows, width)
    with jax.named_scope("kept"):
        top, acc = call(
            kept_kernel,
            "kept",
            [SMEM] + [VMEM] * 4,
            [((GROUP, tok), f32), ((GROUP, AUG, tok), f32)],
            ((host * kept_rows)[None].astype(jnp.int32), queries, kept, top, acc),
            [pltpu.VMEM((AUG, hosts * kept_rows), bf16)],
            flops=4 * GROUP * tok * hosts * kept_rows * HD,
            nbytes=8 << 20,
        )
    with jax.named_scope("anchor"):
        (out,) = call(
            anchor_kernel,
            "anchor",
            [VMEM] * 4,
            [((tok, GROUP * HD), bf16)],
            (queries, anchor, top, acc),
            [pltpu.VMEM((AUG, anchor.shape[0]), bf16), pltpu.VMEM((GROUP, tok), f32)],
            flops=4 * GROUP * tok * anchor.shape[0] * HD,
            nbytes=5 << 20,
        )
    return out


def solution(mesh):
    placed = (
        P("hst", "tensor"),
        P("hst", "tensor"),
        P("hst", "tensor"),
        P(("hst", "tensor"), None),
        P(None, "tensor"),
    )
    return jax.shard_map(
        per_device, mesh=mesh, in_specs=placed, out_specs=P("hst", "tensor"), check_vma=False
    )
```

```python
import functools

import jax
import jax.numpy as jnp
from jax import lax
from jax.experimental import pallas as pl
from jax.experimental.pallas import tpu as pltpu
from jax.sharding import PartitionSpec as P

H = 64
KVH = 8
HD = 128
GROUP = H // KVH
EXP2_SCALE = 1.4426950408889634 / HD**0.5
AUG = HD + 16
KEY_BLOCK = 256
KEPT_BLOCK = 1024
SIDE = 4
HEAD_STEP = 4
SAFE_TOTAL = 2.0**100


def mul_nt(a, b):
    return lax.dot_general(a, b, (((1,), (1,)), ((), ())), preferred_element_type=jnp.float32)


def mul(a, b):
    return lax.dot_general(a, b, (((1,), (0,)), ((), ())), preferred_element_type=jnp.float32)


def weights_of(scores, top):
    return jnp.exp2((scores - top) * EXP2_SCALE).astype(jnp.bfloat16)


def weighted(vt_ref, first, weights):
    total = None
    for i, block in enumerate(weights):
        at = pl.ds(first + i * KEY_BLOCK, KEY_BLOCK)
        if not isinstance(first, int):
            at = pl.ds(pl.multiple_of(first + i * KEY_BLOCK, KEY_BLOCK), KEY_BLOCK)
        term = mul(vt_ref[:, at], block)
        total = term if total is None else total + term
    return total


def head_cols(head):
    if isinstance(head, int):
        return slice(head * HD, (head + 1) * HD)
    return pl.ds(pl.multiple_of(head * HD, HD), HD)


def fill_values(vt_ref, kv_ref):
    vt_ref[:HD, :] = kv_ref[:, HD:].T
    vt_ref[HD:, :] = jnp.ones((AUG - HD, vt_ref.shape[1]), jnp.bfloat16)


def start_all(pairs, sem):
    copies = [pltpu.make_async_copy(src, dst, sem.at[i]) for i, (src, dst) in enumerate(pairs)]
    for copy in copies:
        copy.start()
    return copies


def wait_all(copies):
    for copy in copies:
        copy.wait()


def repeat_kernel(rows_hbm, out_hbm, rows_ref, load_sem, sem):
    wait_all(start_all([(rows_hbm, rows_ref)], load_sem))
    wait_all(start_all([(rows_ref, out_hbm.at[i]) for i in range(out_hbm.shape[0])], sem))


def select_kernel(retain_hbm, own_hbm, kept_hbm, retain_ref, kv_ref, kept_ref, sem):
    load = start_all([(own_hbm, kv_ref), (retain_hbm, retain_ref)], sem)
    tok, kept_rows = kv_ref.shape[0], kept_ref.shape[0]
    load[1].wait()
    picks = retain_ref[...] == lax.broadcasted_iota(jnp.int32, (tok, kept_rows), 0)
    picks = jnp.where(picks, 1.0, 0.0).astype(jnp.bfloat16)
    load[0].wait()
    kept_ref[...] = lax.dot_general(
        picks, kv_ref[...], (((0,), (0,)), ((), ())), preferred_element_type=jnp.float32
    ).astype(jnp.bfloat16)
    wait_all(start_all([(kept_ref, kept_hbm)], sem))


def project_kernel(rows_ref, w_ref, out_hbm, part_ref, sem):
    rows = jnp.concatenate([rows_ref[i] for i in range(rows_ref.shape[0])], axis=0)
    part_ref[...] = mul(rows, w_ref[...]).astype(jnp.bfloat16)
    wait_all(start_all([(part_ref, out_hbm.at[i]) for i in range(out_hbm.shape[0])], sem))


def own_kernel(q_ref, kv_ref, stat_ref, acc_ref, vt_ref):
    tok = kv_ref.shape[0]
    fill_values(vt_ref, kv_ref)
    keys = lax.broadcasted_iota(jnp.int32, (KEY_BLOCK, KEY_BLOCK), 0)
    queries = lax.broadcasted_iota(jnp.int32, (KEY_BLOCK, KEY_BLOCK), 1)
    seen = keys <= queries

    def one_head(head):
        for block in range(tok // KEY_BLOCK):
            at = slice(block * KEY_BLOCK, (block + 1) * KEY_BLOCK)
            q = q_ref[at, head_cols(head)]
            parts = [
                mul_nt(kv_ref[i * KEY_BLOCK : (i + 1) * KEY_BLOCK, :HD], q) for i in range(block + 1)
            ]
            parts[-1] = jnp.where(seen, parts[-1], -1e30)
            top = functools.reduce(
                jnp.maximum, [jnp.max(part, axis=0, keepdims=True) for part in parts]
            )
            weights = [weights_of(part, top) for part in parts]
            acc = weighted(vt_ref, 0, weights)
            stat_ref[0, pl.ds(head, 1), at] = top
            stat_ref[1, pl.ds(head, 1), at] = acc[HD : HD + 1]
            acc_ref[head, :, at] = acc[:HD].astype(jnp.bfloat16)

    def step(i, carry):
        for part in range(HEAD_STEP):
            one_head(HEAD_STEP * i + part)
        return carry

    lax.fori_loop(0, GROUP // HEAD_STEP, step, 0)


def fast_rows(q_ref, kv_ref, vt_ref, stat_ref, head, first, rows):
    q = q_ref[:, head_cols(head)]
    top = stat_ref[0, pl.ds(head, 1), :]
    weights = []
    for i in range(rows // KEY_BLOCK):
        at = pl.ds(first + i * KEY_BLOCK, KEY_BLOCK)
        if not isinstance(first, int):
            at = pl.ds(pl.multiple_of(first + i * KEY_BLOCK, KEY_BLOCK), KEY_BLOCK)
        weights.append(weights_of(mul_nt(kv_ref[at, :HD], q), top))
    return weighted(vt_ref, first, weights)


def careful_rows(q_ref, kv_ref, vt_ref, stat_ref, acc_ref, head, count):
    q = q_ref[:, head_cols(head)]

    def block_step(block, carry):
        top, acc = carry
        at = pl.ds(pl.multiple_of(block * KEY_BLOCK, KEY_BLOCK), KEY_BLOCK)
        row = lax.broadcasted_iota(jnp.int32, (KEY_BLOCK, 1), 0) + block * KEY_BLOCK
        scores = jnp.where(row < count, mul_nt(kv_ref[at, :HD], q), -1e30)
        new_top = jnp.maximum(top, jnp.max(scores, axis=0, keepdims=True))
        term = mul(vt_ref[:, at], weights_of(scores, new_top))
        return new_top, acc * jnp.exp2((top - new_top) * EXP2_SCALE) + term

    total = jnp.broadcast_to(stat_ref[1, pl.ds(head, 1), :], (AUG - HD, q.shape[0]))
    acc = jnp.concatenate([acc_ref[head].astype(jnp.float32), total], axis=0)
    return lax.fori_loop(
        0, kv_ref.shape[0] // KEY_BLOCK, block_step, (stat_ref[0, pl.ds(head, 1), :], acc)
    )


def kept_kernel(
    at_ref,
    q_ref,
    mine_hbm,
    other_hbm,
    stat_ref,
    acc_ref,
    new_stat_ref,
    new_acc_ref,
    mine_ref,
    other_ref,
    sum_ref,
    kv_ref,
    vt_ref,
    sem,
):
    load = start_all([(mine_hbm, mine_ref), (other_hbm, other_ref)], sem)
    for head in range(GROUP):
        sum_ref[head, :HD] = acc_ref[head].astype(jnp.float32)
        sum_ref[head, HD:] = jnp.broadcast_to(
            stat_ref[1, head : head + 1, :], (AUG - HD, sum_ref.shape[2])
        )
    wait_all(load)
    host = at_ref[0]
    chip, core = lax.div(host, 2), lax.rem(host, 2)
    senders, kept_rows, _ = mine_ref.shape
    count = host * kept_rows
    for piece in range(senders):
        y = lax.rem(lax.div(chip, SIDE) + SIDE - piece // SIDE, SIDE)
        x = lax.rem(lax.rem(chip, SIDE) + SIDE - piece % SIDE, SIDE)
        first = (y * SIDE + x) * 2 * kept_rows
        for ref, which in ((mine_ref, core), (other_ref, 1 - core)):
            at = pl.multiple_of(first + which * kept_rows, kept_rows)
            kv_ref[pl.ds(at, kept_rows), :] = ref[piece]
    fill_values(vt_ref, kv_ref)
    spare = lax.broadcasted_iota(jnp.int32, vt_ref.shape, 1) >= count
    vt_ref[...] = jnp.where(spare, 0.0, vt_ref[...]).astype(jnp.bfloat16)
    steps = GROUP // HEAD_STEP

    def step(i, carry):
        first = lax.div(i, steps) * KEPT_BLOCK
        for part in range(HEAD_STEP):
            head = lax.rem(i, steps) * HEAD_STEP + part
            sum_ref[head] += fast_rows(q_ref, kv_ref, vt_ref, stat_ref, head, first, KEPT_BLOCK)
        return carry

    lax.fori_loop(0, lax.div(count + KEPT_BLOCK - 1, KEPT_BLOCK) * steps, step, 0)
    new_stat_ref[0] = stat_ref[0]
    for head in range(GROUP):
        new_acc_ref[head] = sum_ref[head, :HD].astype(jnp.bfloat16)
        new_stat_ref[1, head : head + 1, :] = sum_ref[head, HD : HD + 1]
    safe = jnp.all(new_stat_ref[1] < SAFE_TOTAL)

    @pl.when(jnp.logical_not(safe))
    def careful():
        def head_step(head, carry):
            top, acc = careful_rows(q_ref, kv_ref, vt_ref, stat_ref, acc_ref, head, count)
            new_stat_ref[0, pl.ds(head, 1), :] = top
            new_stat_ref[1, pl.ds(head, 1), :] = acc[HD : HD + 1]
            new_acc_ref[head] = acc[:HD].astype(jnp.bfloat16)
            return carry

        lax.fori_loop(0, GROUP, head_step, 0)


def anchor_kernel(q_ref, kv_ref, stat_ref, acc_ref, out_ref, vt_ref, total_ref):
    fill_values(vt_ref, kv_ref)
    rows = kv_ref.shape[0]

    def finish(head, acc, total):
        out_ref[:, head_cols(head)] = (acc * (1.0 / total)).T.astype(jnp.bfloat16)

    for head in range(GROUP):
        term = fast_rows(q_ref, kv_ref, vt_ref, stat_ref, head, 0, rows)
        total = stat_ref[1, head : head + 1, :] + term[HD : HD + 1]
        total_ref[head : head + 1, :] = total
        finish(head, acc_ref[head].astype(jnp.float32) + term[:HD], total)
    safe = jnp.all(total_ref[...] < SAFE_TOTAL)

    @pl.when(jnp.logical_not(safe))
    def careful():
        def head_step(head, carry):
            _, acc = careful_rows(q_ref, kv_ref, vt_ref, stat_ref, acc_ref, head, rows)
            finish(head, acc[:HD], acc[HD : HD + 1])
            return carry

        lax.fori_loop(0, GROUP, head_step, 0)


VMEM = pl.BlockSpec(memory_space=pltpu.VMEM)
SMEM = pl.BlockSpec(memory_space=pltpu.SMEM)


HBM = pl.BlockSpec(memory_space=pltpu.HBM)


def call(kernel, name, in_specs, outs, args, scratch=(), flops=0, nbytes=0, limit=24, out_spec=VMEM):
    return pl.pallas_call(
        kernel,
        in_specs=in_specs,
        out_specs=[out_spec] * len(outs),
        out_shape=[jax.ShapeDtypeStruct(shape, dtype) for shape, dtype in outs],
        scratch_shapes=list(scratch),
        compiler_params=pltpu.CompilerParams(vmem_limit_bytes=limit << 20),
        cost_estimate=pl.CostEstimate(flops=flops, bytes_accessed=nbytes, transcendentals=0),
        name=name,
    )(*args)


def moves(dy, dx, dcore=0):
    pairs = []
    for y in range(SIDE):
        for x in range(SIDE):
            for core in range(2):
                to = ((y + dy) % SIDE * SIDE + (x + dx) % SIDE) * 2 + (core ^ dcore)
                pairs.append(((y * SIDE + x) * 2 + core, to))
    return pairs


def per_device(queries, own_kv, retain, anchor_hidden, w_kv):
    tok, width = own_kv.shape
    hosts = lax.axis_size("hst")
    heads = lax.axis_size("tensor")
    host = lax.axis_index("hst")
    kept_rows = retain.shape[0]
    rows = anchor_hidden.shape[0]
    bf16, f32 = jnp.bfloat16, jnp.float32
    state = [((2, GROUP, tok), f32), ((GROUP, HD, tok), bf16)]
    barrier = lax.optimization_barrier

    dma = pltpu.SemaphoreType.DMA
    with jax.named_scope("gather_hidden"):
        (hidden,) = call(
            repeat_kernel,
            "repeat",
            [HBM],
            [((heads, *anchor_hidden.shape), bf16)],
            (anchor_hidden,),
            [pltpu.VMEM(anchor_hidden.shape, bf16), dma((1,)), dma((heads,))],
            nbytes=1 << 20,
            limit=63,
            out_spec=HBM,
        )
        hidden, own_kv, queries, retain = barrier((hidden, own_kv, queries, retain))
        hidden = lax.all_to_all(hidden, "tensor", 0, 0)
    with jax.named_scope("select_kept"):
        (kept,) = call(
            select_kernel,
            "select",
            [HBM] * 2,
            [((kept_rows, width), bf16)],
            (retain.T, own_kv),
            [
                pltpu.VMEM((1, kept_rows), jnp.int32),
                pltpu.VMEM((tok, width), bf16),
                pltpu.VMEM((kept_rows, width), bf16),
                dma((2,)),
            ],
            flops=2 * kept_rows * tok * width,
            nbytes=1 << 18,
            limit=63,
            out_spec=HBM,
        )
        kept, own_kv, queries = barrier((kept, own_kv, queries))
        row = [kept] + [lax.ppermute(kept, "hst", moves(0, d)) for d in range(1, SIDE)]

    with jax.named_scope("own"):
        stat, acc = call(
            own_kernel,
            "own",
            [VMEM, VMEM],
            state,
            (queries, own_kv),
            [pltpu.VMEM((AUG, tok), bf16)],
            nbytes=1 << 10,
        )
    with jax.named_scope("kept_rows"):
        *row, stat, acc = barrier((*row, stat, acc))
        row = jnp.stack(row)
        plane = [row] + [lax.ppermute(row, "hst", moves(d, 0)) for d in range(1, SIDE)]
    with jax.named_scope("project"):
        hidden, row, stat, acc = barrier((hidden, row, stat, acc))
        (part,) = call(
            project_kernel,
            "project",
            [VMEM] * 2,
            [((hosts, heads * rows, width), bf16)],
            (hidden, w_kv),
            [pltpu.VMEM((heads * rows, width), bf16), dma((hosts,))],
            flops=2 * heads * rows * w_kv.shape[0] * width,
            nbytes=5 << 20,
            out_spec=HBM,
        )
        _, *plane = barrier((part, *plane))
        anchor = lax.all_to_all(part, "hst", 0, 0).reshape(hosts * heads * rows, width)
        mine = jnp.concatenate(plane)
        other = lax.ppermute(mine, "hst", moves(0, 0, 1))
    with jax.named_scope("kept"):
        stat, acc = call(
            kept_kernel,
            "kept",
            [SMEM, VMEM, HBM, HBM, VMEM, VMEM],
            state,
            (host[None].astype(jnp.int32), queries, mine, other, stat, acc),
            [
                pltpu.VMEM(mine.shape, bf16),
                pltpu.VMEM(mine.shape, bf16),
                pltpu.VMEM((GROUP, AUG, tok), f32),
                pltpu.VMEM((hosts * kept_rows, width), bf16),
                pltpu.VMEM((AUG, hosts * kept_rows), bf16),
                dma((2,)),
            ],
            nbytes=1 << 10,
        )
    with jax.named_scope("anchor"):
        (out,) = call(
            anchor_kernel,
            "anchor",
            [VMEM] * 4,
            [((tok, GROUP * HD), bf16)],
            (queries, anchor, stat, acc),
            [pltpu.VMEM((AUG, anchor.shape[0]), bf16), pltpu.VMEM((GROUP, tok), f32)],
            nbytes=1 << 20,
        )
    return out


def solution(mesh):
    placed = (
        P("hst", "tensor"),
        P("hst", "tensor"),
        P("hst", "tensor"),
        P(("hst", "tensor"), None),
        P(None, "tensor"),
    )
    return jax.shard_map(
        per_device, mesh=mesh, in_specs=placed, out_specs=P("hst", "tensor"), check_vma=False
    )
```

```python
import functools

import jax
import jax.numpy as jnp
from jax import lax
from jax.experimental import pallas as pl
from jax.experimental.pallas import tpu as pltpu
from jax.sharding import PartitionSpec as P

H = 64
KVH = 8
HD = 128
GROUP = H // KVH
EXP2_SCALE = 1.4426950408889634 / HD**0.5
AUG = HD + 16
KEY_BLOCK = 256
KEPT_BLOCK = 1024
SIDE = 4
OWN_FIRST = 6
HEAD_STEP = 4
SAFE_TOTAL = 2.0**100


def mul_nt(a, b):
    return lax.dot_general(a, b, (((1,), (1,)), ((), ())), preferred_element_type=jnp.float32)


def mul(a, b):
    return lax.dot_general(a, b, (((1,), (0,)), ((), ())), preferred_element_type=jnp.float32)


def weights_of(scores, top):
    return jnp.exp2((scores - top) * EXP2_SCALE).astype(jnp.bfloat16)


def weighted(vt_ref, first, weights):
    total = None
    for i, block in enumerate(weights):
        at = pl.ds(first + i * KEY_BLOCK, KEY_BLOCK)
        if not isinstance(first, int):
            at = pl.ds(pl.multiple_of(first + i * KEY_BLOCK, KEY_BLOCK), KEY_BLOCK)
        term = mul(vt_ref[:, at], block)
        total = term if total is None else total + term
    return total


def head_cols(head):
    if isinstance(head, int):
        return slice(head * HD, (head + 1) * HD)
    return pl.ds(pl.multiple_of(head * HD, HD), HD)


def fill_values(vt_ref, kv_ref):
    vt_ref[:HD, :] = kv_ref[:, HD:].T
    vt_ref[HD:, :] = jnp.ones((AUG - HD, vt_ref.shape[1]), jnp.bfloat16)


def start_all(pairs, sem):
    copies = [pltpu.make_async_copy(src, dst, sem.at[i]) for i, (src, dst) in enumerate(pairs)]
    for copy in copies:
        copy.start()
    return copies


def wait_all(copies):
    for copy in copies:
        copy.wait()


def repeat_kernel(rows_hbm, out_hbm, rows_ref, load_sem, sem):
    half = rows_hbm.shape[1] // 2
    parts = [slice(0, half), slice(half, 2 * half)]
    load = start_all([(rows_hbm.at[:, at], rows_ref.at[:, at]) for at in parts], load_sem)
    store = []
    for part, at in enumerate(parts):
        load[part].wait()
        pairs = [(rows_ref.at[:, at], out_hbm.at[i, :, at]) for i in range(out_hbm.shape[0])]
        store += start_all(pairs, sem.at[part])
    wait_all(store)


def select_kernel(retain_hbm, own_hbm, kept_hbm, retain_ref, kv_ref, kept_ref, sem):
    load = start_all([(own_hbm, kv_ref), (retain_hbm, retain_ref)], sem)
    tok, kept_rows = kv_ref.shape[0], kept_ref.shape[0]
    load[1].wait()
    picks = retain_ref[...] == lax.broadcasted_iota(jnp.int32, (tok, kept_rows), 0)
    picks = jnp.where(picks, 1.0, 0.0).astype(jnp.bfloat16)
    load[0].wait()
    kept_ref[...] = lax.dot_general(
        picks, kv_ref[...], (((0,), (0,)), ((), ())), preferred_element_type=jnp.float32
    ).astype(jnp.bfloat16)
    wait_all(start_all([(kept_ref, kept_hbm)], sem))


def project_kernel(rows_ref, w_ref, out_ref):
    rows = jnp.concatenate([rows_ref[i] for i in range(rows_ref.shape[0])], axis=0)
    out_ref[...] = mul(rows, w_ref[...]).astype(jnp.bfloat16)


def own_kernel(first, heads, q_ref, kv_ref, stat_ref, acc_ref, vt_ref):
    tok = kv_ref.shape[0]
    fill_values(vt_ref, kv_ref)
    keys = lax.broadcasted_iota(jnp.int32, (KEY_BLOCK, KEY_BLOCK), 0)
    queries = lax.broadcasted_iota(jnp.int32, (KEY_BLOCK, KEY_BLOCK), 1)
    seen = keys <= queries

    for head in range(heads):
        for block in range(tok // KEY_BLOCK):
            at = slice(block * KEY_BLOCK, (block + 1) * KEY_BLOCK)
            q = q_ref[at, head_cols(first + head)]
            parts = [
                mul_nt(kv_ref[i * KEY_BLOCK : (i + 1) * KEY_BLOCK, :HD], q) for i in range(block + 1)
            ]
            parts[-1] = jnp.where(seen, parts[-1], -1e30)
            top = functools.reduce(
                jnp.maximum, [jnp.max(part, axis=0, keepdims=True) for part in parts]
            )
            acc = weighted(vt_ref, 0, [weights_of(part, top) for part in parts])
            stat_ref[0, head : head + 1, at] = top
            stat_ref[1, head : head + 1, at] = acc[HD : HD + 1]
            acc_ref[head, :, at] = acc[:HD].astype(jnp.bfloat16)


def fast_rows(q_ref, kv_ref, vt_ref, stat_ref, head, first, rows):
    q = q_ref[:, head_cols(head)]
    top = stat_ref[0, pl.ds(head, 1), :]
    weights = []
    for i in range(rows // KEY_BLOCK):
        at = pl.ds(first + i * KEY_BLOCK, KEY_BLOCK)
        if not isinstance(first, int):
            at = pl.ds(pl.multiple_of(first + i * KEY_BLOCK, KEY_BLOCK), KEY_BLOCK)
        weights.append(weights_of(mul_nt(kv_ref[at, :HD], q), top))
    return weighted(vt_ref, first, weights)


def careful_rows(q_ref, kv_ref, vt_ref, stat_ref, acc_ref, head, count):
    q = q_ref[:, head_cols(head)]

    def block_step(block, carry):
        top, acc = carry
        at = pl.ds(pl.multiple_of(block * KEY_BLOCK, KEY_BLOCK), KEY_BLOCK)
        row = lax.broadcasted_iota(jnp.int32, (KEY_BLOCK, 1), 0) + block * KEY_BLOCK
        scores = jnp.where(row < count, mul_nt(kv_ref[at, :HD], q), -1e30)
        new_top = jnp.maximum(top, jnp.max(scores, axis=0, keepdims=True))
        term = mul(vt_ref[:, at], weights_of(scores, new_top))
        return new_top, acc * jnp.exp2((top - new_top) * EXP2_SCALE) + term

    total = jnp.broadcast_to(stat_ref[1, pl.ds(head, 1), :], (AUG - HD, q.shape[0]))
    acc = jnp.concatenate([acc_ref[head].astype(jnp.float32), total], axis=0)
    return lax.fori_loop(
        0, kv_ref.shape[0] // KEY_BLOCK, block_step, (stat_ref[0, pl.ds(head, 1), :], acc)
    )


def kept_kernel(
    at_ref,
    q_ref,
    mine_ref,
    other_ref,
    stat_a_ref,
    acc_a_ref,
    stat_b_ref,
    acc_b_ref,
    new_stat_ref,
    new_acc_ref,
    stat_ref,
    own_ref,
    sum_ref,
    kv_ref,
    vt_ref,
):
    first = 0
    for stat_part, acc_part in ((stat_a_ref, acc_a_ref), (stat_b_ref, acc_b_ref)):
        heads = acc_part.shape[0]
        stat_ref[:, first : first + heads] = stat_part[...]
        for head in range(heads):
            sum_ref[first + head, :HD] = acc_part[head].astype(jnp.float32)
            total = stat_part[1, head : head + 1, :]
            sum_ref[first + head, HD:] = jnp.broadcast_to(total, (AUG - HD, sum_ref.shape[2]))
        first += heads
    host = at_ref[0]
    chip, core = lax.div(host, 2), lax.rem(host, 2)
    senders, kept_rows, _ = mine_ref.shape
    count = host * kept_rows
    for piece in range(senders):
        y = lax.rem(lax.div(chip, SIDE) + SIDE - piece // SIDE, SIDE)
        x = lax.rem(lax.rem(chip, SIDE) + SIDE - piece % SIDE, SIDE)
        first = (y * SIDE + x) * 2 * kept_rows
        for ref, which in ((mine_ref, core), (other_ref, 1 - core)):
            at = pl.multiple_of(first + which * kept_rows, kept_rows)
            kv_ref[pl.ds(at, kept_rows), :] = ref[piece]
    fill_values(vt_ref, kv_ref)
    spare = lax.broadcasted_iota(jnp.int32, vt_ref.shape, 1) >= count
    vt_ref[...] = jnp.where(spare, 0.0, vt_ref[...]).astype(jnp.bfloat16)
    steps = GROUP // HEAD_STEP

    def step(i, carry):
        first = lax.div(i, steps) * KEPT_BLOCK
        for part in range(HEAD_STEP):
            head = lax.rem(i, steps) * HEAD_STEP + part
            sum_ref[head] += fast_rows(q_ref, kv_ref, vt_ref, stat_ref, head, first, KEPT_BLOCK)
        return carry

    lax.fori_loop(0, lax.div(count + KEPT_BLOCK - 1, KEPT_BLOCK) * steps, step, 0)
    new_stat_ref[0] = stat_ref[0]
    for head in range(GROUP):
        new_acc_ref[head] = sum_ref[head, :HD].astype(jnp.bfloat16)
        new_stat_ref[1, head : head + 1, :] = sum_ref[head, HD : HD + 1]
    safe = jnp.all(new_stat_ref[1] < SAFE_TOTAL)

    @pl.when(jnp.logical_not(safe))
    def careful():
        own_ref[:OWN_FIRST] = acc_a_ref[...]
        own_ref[OWN_FIRST:] = acc_b_ref[...]

        def head_step(head, carry):
            top, acc = careful_rows(q_ref, kv_ref, vt_ref, stat_ref, own_ref, head, count)
            new_stat_ref[0, pl.ds(head, 1), :] = top
            new_stat_ref[1, pl.ds(head, 1), :] = acc[HD : HD + 1]
            new_acc_ref[head] = acc[:HD].astype(jnp.bfloat16)
            return carry

        lax.fori_loop(0, GROUP, head_step, 0)


def anchor_kernel(q_ref, kv_ref, stat_ref, acc_ref, out_ref, vt_ref, total_ref):
    fill_values(vt_ref, kv_ref)
    rows = kv_ref.shape[0]

    def finish(head, acc, total):
        out_ref[:, head_cols(head)] = (acc * (1.0 / total)).T.astype(jnp.bfloat16)

    for head in range(GROUP):
        term = fast_rows(q_ref, kv_ref, vt_ref, stat_ref, head, 0, rows)
        total = stat_ref[1, head : head + 1, :] + term[HD : HD + 1]
        total_ref[head : head + 1, :] = total
        finish(head, acc_ref[head].astype(jnp.float32) + term[:HD], total)
    safe = jnp.all(total_ref[...] < SAFE_TOTAL)

    @pl.when(jnp.logical_not(safe))
    def careful():
        def head_step(head, carry):
            _, acc = careful_rows(q_ref, kv_ref, vt_ref, stat_ref, acc_ref, head, rows)
            finish(head, acc[:HD], acc[HD : HD + 1])
            return carry

        lax.fori_loop(0, GROUP, head_step, 0)


VMEM = pl.BlockSpec(memory_space=pltpu.VMEM)
SMEM = pl.BlockSpec(memory_space=pltpu.SMEM)


HBM = pl.BlockSpec(memory_space=pltpu.HBM)


def call(kernel, name, in_specs, outs, args, scratch=(), flops=0, nbytes=0, limit=24, out_spec=VMEM):
    return pl.pallas_call(
        kernel,
        in_specs=in_specs,
        out_specs=[out_spec] * len(outs),
        out_shape=[jax.ShapeDtypeStruct(shape, dtype) for shape, dtype in outs],
        scratch_shapes=list(scratch),
        compiler_params=pltpu.CompilerParams(vmem_limit_bytes=limit << 20),
        cost_estimate=pl.CostEstimate(flops=flops, bytes_accessed=nbytes, transcendentals=0),
        name=name,
    )(*args)


def moves(dy, dx, dcore=0):
    pairs = []
    for y in range(SIDE):
        for x in range(SIDE):
            for core in range(2):
                to = ((y + dy) % SIDE * SIDE + (x + dx) % SIDE) * 2 + (core ^ dcore)
                pairs.append(((y * SIDE + x) * 2 + core, to))
    return pairs


def per_device(queries, own_kv, retain, anchor_hidden, w_kv):
    tok, width = own_kv.shape
    hosts = lax.axis_size("hst")
    heads = lax.axis_size("tensor")
    host = lax.axis_index("hst")
    kept_rows = retain.shape[0]
    rows = anchor_hidden.shape[0]
    bf16, f32 = jnp.bfloat16, jnp.float32
    state = [((2, GROUP, tok), f32), ((GROUP, HD, tok), bf16)]
    barrier = lax.optimization_barrier

    dma = pltpu.SemaphoreType.DMA

    def own(first, count, weight, queries, own_kv):
        return call(
            functools.partial(own_kernel, first, count),
            "own",
            [VMEM] * 2,
            [((2, count, tok), f32), ((count, HD, tok), bf16)],
            (queries, own_kv),
            [pltpu.VMEM((AUG, tok), bf16)],
            flops=weight * GROUP * tok * tok * HD,
            nbytes=1 << 10,
        )

    with jax.named_scope("gather_hidden"):
        (hidden,) = call(
            repeat_kernel,
            "repeat",
            [HBM],
            [((heads, *anchor_hidden.shape), bf16)],
            (anchor_hidden,),
            [pltpu.VMEM(anchor_hidden.shape, bf16), dma((2,)), dma((2, heads))],
            nbytes=1 << 20,
            limit=63,
            out_spec=HBM,
        )
        hidden, own_kv, queries, retain = barrier((hidden, own_kv, queries, retain))
        hidden = lax.all_to_all(hidden, "tensor", 0, 0)
    with jax.named_scope("select_kept"):
        (kept,) = call(
            select_kernel,
            "select",
            [HBM] * 2,
            [((kept_rows, width), bf16)],
            (retain.T, own_kv),
            [
                pltpu.VMEM((1, kept_rows), jnp.int32),
                pltpu.VMEM((tok, width), bf16),
                pltpu.VMEM((kept_rows, width), bf16),
                dma((2,)),
            ],
            flops=2 * kept_rows * tok * width,
            nbytes=1 << 18,
            limit=63,
            out_spec=HBM,
        )
        kept, own_kv, queries = barrier((kept, own_kv, queries))
        row = [kept] + [lax.ppermute(kept, "hst", moves(0, d)) for d in range(1, SIDE)]
        own_a = own(0, OWN_FIRST, 0, queries, own_kv)
        *row, stat_a, acc_a = barrier((*row, *own_a))
        row = jnp.stack(row)
        plane = [row] + [lax.ppermute(row, "hst", moves(d, 0)) for d in range(1, SIDE)]
    with jax.named_scope("project"):
        hidden, row = barrier((hidden, row))
        (part,) = call(
            project_kernel,
            "project",
            [VMEM] * 2,
            [((heads * rows, width), bf16)],
            (hidden, w_kv),
            flops=2 * heads * rows * w_kv.shape[0] * width,
            nbytes=5 << 20,
        )
        part = jnp.concatenate([part, lax.ppermute(part, "hst", moves(0, 0, 1))])
        part = jnp.broadcast_to(part[None], (hosts // 2, *part.shape))
        _, own_kv, queries, *plane = barrier((part, own_kv, queries, *plane))
        same_core = [[2 * chip + core for chip in range(hosts // 2)] for core in range(2)]
        anchor = lax.all_to_all(part, "hst", 0, 0, axis_index_groups=same_core)
        anchor = anchor.reshape(hosts * heads * rows, width)
        mine = jnp.concatenate(plane)
        other = lax.ppermute(mine, "hst", moves(0, 0, 1))
    with jax.named_scope("own"):
        stat_b, acc_b = own(OWN_FIRST, GROUP - OWN_FIRST, 320, queries, own_kv)
    with jax.named_scope("kept"):
        stat, acc = call(
            kept_kernel,
            "kept",
            [SMEM] + [VMEM] * 7,
            state,
            (host[None].astype(jnp.int32), queries, mine, other, stat_a, acc_a, stat_b, acc_b),
            [
                *(pltpu.VMEM(*one) for one in state),
                pltpu.VMEM((GROUP, AUG, tok), f32),
                pltpu.VMEM((hosts * kept_rows, width), bf16),
                pltpu.VMEM((AUG, hosts * kept_rows), bf16),
            ],
            flops=4 * GROUP * tok * hosts * kept_rows * HD,
            nbytes=8 << 20,
        )
    with jax.named_scope("anchor"):
        (out,) = call(
            anchor_kernel,
            "anchor",
            [VMEM] * 4,
            [((tok, GROUP * HD), bf16)],
            (queries, anchor, stat, acc),
            [pltpu.VMEM((AUG, anchor.shape[0]), bf16), pltpu.VMEM((GROUP, tok), f32)],
            nbytes=1 << 20,
        )
    return out


def solution(mesh):
    placed = (
        P("hst", "tensor"),
        P("hst", "tensor"),
        P("hst", "tensor"),
        P(("hst", "tensor"), None),
        P(None, "tensor"),
    )
    return jax.shard_map(
        per_device, mesh=mesh, in_specs=placed, out_specs=P("hst", "tensor"), check_vma=False
    )
```

```python
import functools

import jax
import jax.numpy as jnp
from jax import lax
from jax.experimental import pallas as pl
from jax.experimental.pallas import tpu as pltpu
from jax.sharding import PartitionSpec as P

H = 64
KVH = 8
HD = 128
GROUP = H // KVH
EXP2_SCALE = 1.4426950408889634 / HD**0.5
AUG = HD + 16
KEY_BLOCK = 256
KEPT_BLOCK = 1024
SIDE = 4
OWN_FIRST = 6
HEAD_STEP = 8
SAFE_TOTAL = 2.0**100


def mul_nt(a, b):
    return lax.dot_general(a, b, (((1,), (1,)), ((), ())), preferred_element_type=jnp.float32)


def mul(a, b):
    return lax.dot_general(a, b, (((1,), (0,)), ((), ())), preferred_element_type=jnp.float32)


def weights_of(scores, top):
    return jnp.exp2((scores - top) * EXP2_SCALE).astype(jnp.bfloat16)


def weighted(vt_ref, first, weights):
    total = None
    for i, block in enumerate(weights):
        at = pl.ds(first + i * KEY_BLOCK, KEY_BLOCK)
        if not isinstance(first, int):
            at = pl.ds(pl.multiple_of(first + i * KEY_BLOCK, KEY_BLOCK), KEY_BLOCK)
        term = mul(vt_ref[:, at], block)
        total = term if total is None else total + term
    return total


def head_cols(head):
    if isinstance(head, int):
        return slice(head * HD, (head + 1) * HD)
    return pl.ds(pl.multiple_of(head * HD, HD), HD)


def fill_values(vt_ref, kv_ref):
    vt_ref[:HD, :] = kv_ref[:, HD:].T
    vt_ref[HD:, :] = jnp.ones((AUG - HD, vt_ref.shape[1]), jnp.bfloat16)


def start_all(pairs, sem):
    copies = [pltpu.make_async_copy(src, dst, sem.at[i]) for i, (src, dst) in enumerate(pairs)]
    for copy in copies:
        copy.start()
    return copies


def wait_all(copies):
    for copy in copies:
        copy.wait()


def repeat_kernel(rows_hbm, out_hbm, rows_ref, load_sem, sem):
    half = rows_hbm.shape[1] // 2
    parts = [slice(0, half), slice(half, 2 * half)]
    load = start_all([(rows_hbm.at[:, at], rows_ref.at[:, at]) for at in parts], load_sem)
    store = []
    for part, at in enumerate(parts):
        load[part].wait()
        pairs = [(rows_ref.at[:, at], out_hbm.at[i, :, at]) for i in range(out_hbm.shape[0])]
        store += start_all(pairs, sem.at[part])
    wait_all(store)


def select_kernel(retain_hbm, own_hbm, kept_hbm, retain_ref, kv_ref, kept_ref, sem):
    load = start_all([(own_hbm, kv_ref), (retain_hbm, retain_ref)], sem)
    tok, kept_rows = kv_ref.shape[0], kept_ref.shape[0]
    load[1].wait()
    picks = retain_ref[...] == lax.broadcasted_iota(jnp.int32, (tok, kept_rows), 0)
    picks = jnp.where(picks, 1.0, 0.0).astype(jnp.bfloat16)
    load[0].wait()
    kept_ref[...] = lax.dot_general(
        picks, kv_ref[...], (((0,), (0,)), ((), ())), preferred_element_type=jnp.float32
    ).astype(jnp.bfloat16)
    wait_all(start_all([(kept_ref, kept_hbm)], sem))


def project_kernel(rows_ref, w_ref, out_ref):
    rows = jnp.concatenate([rows_ref[i] for i in range(rows_ref.shape[0])], axis=0)
    out_ref[...] = mul(rows, w_ref[...]).astype(jnp.bfloat16)


def own_kernel(first, heads, q_ref, kv_ref, stat_ref, acc_ref, vt_ref):
    tok = kv_ref.shape[0]
    fill_values(vt_ref, kv_ref)
    keys = lax.broadcasted_iota(jnp.int32, (KEY_BLOCK, KEY_BLOCK), 0)
    queries = lax.broadcasted_iota(jnp.int32, (KEY_BLOCK, KEY_BLOCK), 1)
    seen = keys <= queries

    for head in range(heads):
        for block in range(tok // KEY_BLOCK):
            at = slice(block * KEY_BLOCK, (block + 1) * KEY_BLOCK)
            q = q_ref[at, head_cols(first + head)]
            parts = [
                mul_nt(kv_ref[i * KEY_BLOCK : (i + 1) * KEY_BLOCK, :HD], q) for i in range(block + 1)
            ]
            parts[-1] = jnp.where(seen, parts[-1], -1e30)
            top = functools.reduce(
                jnp.maximum, [jnp.max(part, axis=0, keepdims=True) for part in parts]
            )
            acc = weighted(vt_ref, 0, [weights_of(part, top) for part in parts])
            stat_ref[0, head : head + 1, at] = top
            stat_ref[1, head : head + 1, at] = acc[HD : HD + 1]
            acc_ref[head, :, at] = acc[:HD].astype(jnp.bfloat16)


def fast_rows(q_ref, kv_ref, vt_ref, stat_ref, head, first, rows):
    q = q_ref[:, head_cols(head)]
    top = stat_ref[0, pl.ds(head, 1), :]
    weights = []
    for i in range(rows // KEY_BLOCK):
        at = pl.ds(first + i * KEY_BLOCK, KEY_BLOCK)
        if not isinstance(first, int):
            at = pl.ds(pl.multiple_of(first + i * KEY_BLOCK, KEY_BLOCK), KEY_BLOCK)
        weights.append(weights_of(mul_nt(kv_ref[at, :HD], q), top))
    return weighted(vt_ref, first, weights)


def careful_rows(q_ref, kv_ref, vt_ref, stat_ref, acc_ref, head, count):
    q = q_ref[:, head_cols(head)]

    def block_step(block, carry):
        top, acc = carry
        at = pl.ds(pl.multiple_of(block * KEY_BLOCK, KEY_BLOCK), KEY_BLOCK)
        row = lax.broadcasted_iota(jnp.int32, (KEY_BLOCK, 1), 0) + block * KEY_BLOCK
        scores = jnp.where(row < count, mul_nt(kv_ref[at, :HD], q), -1e30)
        new_top = jnp.maximum(top, jnp.max(scores, axis=0, keepdims=True))
        term = mul(vt_ref[:, at], weights_of(scores, new_top))
        return new_top, acc * jnp.exp2((top - new_top) * EXP2_SCALE) + term

    total = jnp.broadcast_to(stat_ref[1, pl.ds(head, 1), :], (AUG - HD, q.shape[0]))
    acc = jnp.concatenate([acc_ref[head].astype(jnp.float32), total], axis=0)
    return lax.fori_loop(
        0, kv_ref.shape[0] // KEY_BLOCK, block_step, (stat_ref[0, pl.ds(head, 1), :], acc)
    )


def kept_kernel(
    at_ref,
    q_ref,
    mine_ref,
    other_ref,
    stat_a_ref,
    acc_a_ref,
    stat_b_ref,
    acc_b_ref,
    new_stat_ref,
    new_acc_ref,
    stat_ref,
    own_ref,
    sum_ref,
    kv_ref,
    vt_ref,
):
    first = 0
    for stat_part, acc_part in ((stat_a_ref, acc_a_ref), (stat_b_ref, acc_b_ref)):
        heads = acc_part.shape[0]
        stat_ref[:, first : first + heads] = stat_part[...]
        for head in range(heads):
            sum_ref[first + head, :HD] = acc_part[head].astype(jnp.float32)
            total = stat_part[1, head : head + 1, :]
            sum_ref[first + head, HD:] = jnp.broadcast_to(total, (AUG - HD, sum_ref.shape[2]))
        first += heads
    host = at_ref[0]
    chip, core = lax.div(host, 2), lax.rem(host, 2)
    senders, kept_rows, _ = mine_ref.shape
    count = host * kept_rows
    for piece in range(senders):
        y = lax.rem(lax.div(chip, SIDE) + SIDE - piece // SIDE, SIDE)
        x = lax.rem(lax.rem(chip, SIDE) + SIDE - piece % SIDE, SIDE)
        first = (y * SIDE + x) * 2 * kept_rows
        for ref, which in ((mine_ref, core), (other_ref, 1 - core)):
            at = pl.multiple_of(first + which * kept_rows, kept_rows)
            kv_ref[pl.ds(at, kept_rows), :] = ref[piece]
    fill_values(vt_ref, kv_ref)
    spare = lax.broadcasted_iota(jnp.int32, vt_ref.shape, 1) >= count
    vt_ref[...] = jnp.where(spare, 0.0, vt_ref[...]).astype(jnp.bfloat16)
    steps = GROUP // HEAD_STEP

    def step(i, carry):
        first = lax.div(i, steps) * KEPT_BLOCK
        for part in range(HEAD_STEP):
            head = lax.rem(i, steps) * HEAD_STEP + part
            sum_ref[head] += fast_rows(q_ref, kv_ref, vt_ref, stat_ref, head, first, KEPT_BLOCK)
        return carry

    lax.fori_loop(0, lax.div(count + KEPT_BLOCK - 1, KEPT_BLOCK) * steps, step, 0)
    new_stat_ref[0] = stat_ref[0]
    for head in range(GROUP):
        new_acc_ref[head] = sum_ref[head, :HD].astype(jnp.bfloat16)
        new_stat_ref[1, head : head + 1, :] = sum_ref[head, HD : HD + 1]
    safe = jnp.all(new_stat_ref[1] < SAFE_TOTAL)

    @pl.when(jnp.logical_not(safe))
    def careful():
        own_ref[:OWN_FIRST] = acc_a_ref[...]
        own_ref[OWN_FIRST:] = acc_b_ref[...]

        def head_step(head, carry):
            top, acc = careful_rows(q_ref, kv_ref, vt_ref, stat_ref, own_ref, head, count)
            new_stat_ref[0, pl.ds(head, 1), :] = top
            new_stat_ref[1, pl.ds(head, 1), :] = acc[HD : HD + 1]
            new_acc_ref[head] = acc[:HD].astype(jnp.bfloat16)
            return carry

        lax.fori_loop(0, GROUP, head_step, 0)


def anchor_kernel(
    q_ref, kv_ref, stat_ref, acc_ref, out_hbm, out_ref, vt_ref, total_ref, sem
):
    fill_values(vt_ref, kv_ref)
    rows = kv_ref.shape[0]

    def store(head):
        return pltpu.make_async_copy(
            out_ref.at[head], out_hbm.at[:, head_cols(head)], sem.at[head]
        )

    def finish(head, acc, total):
        out_ref[head] = (acc * (1.0 / total)).T.astype(jnp.bfloat16)
        store(head).start()

    for head in range(GROUP):
        term = fast_rows(q_ref, kv_ref, vt_ref, stat_ref, head, 0, rows)
        total = stat_ref[1, head : head + 1, :] + term[HD : HD + 1]
        total_ref[head : head + 1, :] = total
        finish(head, acc_ref[head].astype(jnp.float32) + term[:HD], total)
    wait_all([store(head) for head in range(GROUP)])
    safe = jnp.all(total_ref[...] < SAFE_TOTAL)

    @pl.when(jnp.logical_not(safe))
    def careful():
        def head_step(head, carry):
            _, acc = careful_rows(q_ref, kv_ref, vt_ref, stat_ref, acc_ref, head, rows)
            finish(head, acc[:HD], acc[HD : HD + 1])
            store(head).wait()
            return carry

        lax.fori_loop(0, GROUP, head_step, 0)


VMEM = pl.BlockSpec(memory_space=pltpu.VMEM)
SMEM = pl.BlockSpec(memory_space=pltpu.SMEM)


HBM = pl.BlockSpec(memory_space=pltpu.HBM)


def call(kernel, name, in_specs, outs, args, scratch=(), flops=0, nbytes=0, limit=24, out_spec=VMEM):
    return pl.pallas_call(
        kernel,
        in_specs=in_specs,
        out_specs=[out_spec] * len(outs),
        out_shape=[jax.ShapeDtypeStruct(shape, dtype) for shape, dtype in outs],
        scratch_shapes=list(scratch),
        compiler_params=pltpu.CompilerParams(vmem_limit_bytes=limit << 20),
        cost_estimate=pl.CostEstimate(flops=flops, bytes_accessed=nbytes, transcendentals=0),
        name=name,
    )(*args)


def moves(dy, dx, dcore=0):
    pairs = []
    for y in range(SIDE):
        for x in range(SIDE):
            for core in range(2):
                to = ((y + dy) % SIDE * SIDE + (x + dx) % SIDE) * 2 + (core ^ dcore)
                pairs.append(((y * SIDE + x) * 2 + core, to))
    return pairs


def per_device(queries, own_kv, retain, anchor_hidden, w_kv):
    tok, width = own_kv.shape
    hosts = lax.axis_size("hst")
    heads = lax.axis_size("tensor")
    host = lax.axis_index("hst")
    kept_rows = retain.shape[0]
    rows = anchor_hidden.shape[0]
    bf16, f32 = jnp.bfloat16, jnp.float32
    state = [((2, GROUP, tok), f32), ((GROUP, HD, tok), bf16)]
    barrier = lax.optimization_barrier

    dma = pltpu.SemaphoreType.DMA

    def own(first, count, weight, queries, own_kv):
        return call(
            functools.partial(own_kernel, first, count),
            "own",
            [VMEM] * 2,
            [((2, count, tok), f32), ((count, HD, tok), bf16)],
            (queries, own_kv),
            [pltpu.VMEM((AUG, tok), bf16)],
            flops=weight * GROUP * tok * tok * HD,
            nbytes=1 << 10,
        )

    with jax.named_scope("gather_hidden"):
        (hidden,) = call(
            repeat_kernel,
            "repeat",
            [HBM],
            [((heads, *anchor_hidden.shape), bf16)],
            (anchor_hidden,),
            [pltpu.VMEM(anchor_hidden.shape, bf16), dma((2,)), dma((2, heads))],
            nbytes=1 << 20,
            limit=63,
            out_spec=HBM,
        )
        hidden, own_kv, queries, retain = barrier((hidden, own_kv, queries, retain))
        hidden = lax.all_to_all(hidden, "tensor", 0, 0)
    with jax.named_scope("select_kept"):
        (kept,) = call(
            select_kernel,
            "select",
            [HBM] * 2,
            [((kept_rows, width), bf16)],
            (retain.T, own_kv),
            [
                pltpu.VMEM((1, kept_rows), jnp.int32),
                pltpu.VMEM((tok, width), bf16),
                pltpu.VMEM((kept_rows, width), bf16),
                dma((2,)),
            ],
            flops=2 * kept_rows * tok * width,
            nbytes=1 << 18,
            limit=63,
            out_spec=HBM,
        )
        kept, own_kv, queries = barrier((kept, own_kv, queries))
        row = [kept] + [lax.ppermute(kept, "hst", moves(0, d)) for d in range(1, SIDE)]
        own_a = own(0, OWN_FIRST, 0, queries, own_kv)
        *row, stat_a, acc_a = barrier((*row, *own_a))
        row = jnp.stack(row)
        plane = [row] + [lax.ppermute(row, "hst", moves(d, 0)) for d in range(1, SIDE)]
    with jax.named_scope("project"):
        hidden, row = barrier((hidden, row))
        (part,) = call(
            project_kernel,
            "project",
            [VMEM] * 2,
            [((heads * rows, width), bf16)],
            (hidden, w_kv),
            flops=2 * heads * rows * w_kv.shape[0] * width,
            nbytes=5 << 20,
        )
        part = jnp.concatenate([part, lax.ppermute(part, "hst", moves(0, 0, 1))])
        part = jnp.broadcast_to(part[None], (hosts // 2, *part.shape))
        _, own_kv, queries, *plane = barrier((part, own_kv, queries, *plane))
        same_core = [[2 * chip + core for chip in range(hosts // 2)] for core in range(2)]
        anchor = lax.all_to_all(part, "hst", 0, 0, axis_index_groups=same_core)
        anchor = anchor.reshape(hosts * heads * rows, width)
        mine = jnp.concatenate(plane)
        other = lax.ppermute(mine, "hst", moves(0, 0, 1))
    with jax.named_scope("own"):
        stat_b, acc_b = own(OWN_FIRST, GROUP - OWN_FIRST, 320, queries, own_kv)
    with jax.named_scope("kept"):
        stat, acc = call(
            kept_kernel,
            "kept",
            [SMEM] + [VMEM] * 7,
            state,
            (host[None].astype(jnp.int32), queries, mine, other, stat_a, acc_a, stat_b, acc_b),
            [
                *(pltpu.VMEM(*one) for one in state),
                pltpu.VMEM((GROUP, AUG, tok), f32),
                pltpu.VMEM((hosts * kept_rows, width), bf16),
                pltpu.VMEM((AUG, hosts * kept_rows), bf16),
            ],
            flops=4 * GROUP * tok * hosts * kept_rows * HD,
            nbytes=8 << 20,
        )
    with jax.named_scope("anchor"):
        (out,) = call(
            anchor_kernel,
            "anchor",
            [VMEM] * 4,
            [((tok, GROUP * HD), bf16)],
            (queries, anchor, stat, acc),
            [
                pltpu.VMEM((GROUP, tok, HD), bf16),
                pltpu.VMEM((AUG, anchor.shape[0]), bf16),
                pltpu.VMEM((GROUP, tok), f32),
                dma((GROUP,)),
            ],
            out_spec=HBM,
            nbytes=1 << 20,
        )
    return out


def solution(mesh):
    placed = (
        P("hst", "tensor"),
        P("hst", "tensor"),
        P("hst", "tensor"),
        P(("hst", "tensor"), None),
        P(None, "tensor"),
    )
    return jax.shard_map(
        per_device, mesh=mesh, in_specs=placed, out_specs=P("hst", "tensor"), check_vma=False
    )
```

```python
import functools

import jax
import jax.numpy as jnp
from jax import lax
from jax.experimental import pallas as pl
from jax.experimental.pallas import tpu as pltpu
from jax.sharding import PartitionSpec as P

H = 64
KVH = 8
HD = 128
GROUP = H // KVH
EXP2_SCALE = 1.4426950408889634 / HD**0.5
AUG = HD + 16
KEY_BLOCK = 256
KEPT_BLOCK = 1024
SIDE = 4
OWN_FIRST = 7
HEAD_STEP = 8
SAFE_TOTAL = 2.0**100


def mul_nt(a, b):
    return lax.dot_general(a, b, (((1,), (1,)), ((), ())), preferred_element_type=jnp.float32)


def mul(a, b):
    return lax.dot_general(a, b, (((1,), (0,)), ((), ())), preferred_element_type=jnp.float32)


def weights_of(scores, top):
    return jnp.exp2((scores - top) * EXP2_SCALE).astype(jnp.bfloat16)


def weighted(vt_ref, first, weights):
    total = None
    for i, block in enumerate(weights):
        at = pl.ds(first + i * KEY_BLOCK, KEY_BLOCK)
        if not isinstance(first, int):
            at = pl.ds(pl.multiple_of(first + i * KEY_BLOCK, KEY_BLOCK), KEY_BLOCK)
        term = mul(vt_ref[:, at], block)
        total = term if total is None else total + term
    return total


def head_cols(head):
    if isinstance(head, int):
        return slice(head * HD, (head + 1) * HD)
    return pl.ds(pl.multiple_of(head * HD, HD), HD)


def fill_values(vt_ref, kv_ref):
    vt_ref[:HD, :] = kv_ref[:, HD:].T
    vt_ref[HD:, :] = jnp.ones((AUG - HD, vt_ref.shape[1]), jnp.bfloat16)


def start_all(pairs, sem):
    copies = [pltpu.make_async_copy(src, dst, sem.at[i]) for i, (src, dst) in enumerate(pairs)]
    for copy in copies:
        copy.start()
    return copies


def wait_all(copies):
    for copy in copies:
        copy.wait()


def repeat_kernel(rows_hbm, out_hbm, rows_ref, load_sem, sem):
    half = rows_hbm.shape[1] // 2
    parts = [slice(0, half), slice(half, 2 * half)]
    load = start_all([(rows_hbm.at[:, at], rows_ref.at[:, at]) for at in parts], load_sem)
    store = []
    for part, at in enumerate(parts):
        load[part].wait()
        pairs = [(rows_ref.at[:, at], out_hbm.at[i, :, at]) for i in range(out_hbm.shape[0])]
        store += start_all(pairs, sem.at[part])
    wait_all(store)


def select_kernel(retain_hbm, own_hbm, kept_hbm, retain_ref, kv_ref, kept_ref, sem):
    load = start_all([(own_hbm, kv_ref), (retain_hbm, retain_ref)], sem)
    tok, kept_rows = kv_ref.shape[0], kept_ref.shape[0]
    load[1].wait()
    picks = retain_ref[...] == lax.broadcasted_iota(jnp.int32, (tok, kept_rows), 0)
    picks = jnp.where(picks, 1.0, 0.0).astype(jnp.bfloat16)
    load[0].wait()
    kept_ref[...] = lax.dot_general(
        picks, kv_ref[...], (((0,), (0,)), ((), ())), preferred_element_type=jnp.float32
    ).astype(jnp.bfloat16)
    wait_all(start_all([(kept_ref, kept_hbm)], sem))


def project_kernel(rows_ref, w_ref, out_ref):
    rows = jnp.concatenate([rows_ref[i] for i in range(rows_ref.shape[0])], axis=0)
    out_ref[...] = mul(rows, w_ref[...]).astype(jnp.bfloat16)


def own_kernel(first, heads, q_ref, kv_ref, stat_ref, acc_ref, vt_ref):
    tok = kv_ref.shape[0]
    fill_values(vt_ref, kv_ref)
    keys = lax.broadcasted_iota(jnp.int32, (KEY_BLOCK, KEY_BLOCK), 0)
    queries = lax.broadcasted_iota(jnp.int32, (KEY_BLOCK, KEY_BLOCK), 1)
    seen = keys <= queries

    for head in range(heads):
        for block in range(tok // KEY_BLOCK):
            at = slice(block * KEY_BLOCK, (block + 1) * KEY_BLOCK)
            q = q_ref[at, head_cols(first + head)]
            parts = [
                mul_nt(kv_ref[i * KEY_BLOCK : (i + 1) * KEY_BLOCK, :HD], q) for i in range(block + 1)
            ]
            parts[-1] = jnp.where(seen, parts[-1], -1e30)
            top = functools.reduce(
                jnp.maximum, [jnp.max(part, axis=0, keepdims=True) for part in parts]
            )
            acc = weighted(vt_ref, 0, [weights_of(part, top) for part in parts])
            stat_ref[0, head : head + 1, at] = top
            stat_ref[1, head : head + 1, at] = acc[HD : HD + 1]
            acc_ref[head, :, at] = acc[:HD].astype(jnp.bfloat16)


def fast_rows(q_ref, kv_ref, vt_ref, stat_ref, head, first, rows):
    q = q_ref[:, head_cols(head)]
    top = stat_ref[0, pl.ds(head, 1), :]
    weights = []
    for i in range(rows // KEY_BLOCK):
        at = pl.ds(first + i * KEY_BLOCK, KEY_BLOCK)
        if not isinstance(first, int):
            at = pl.ds(pl.multiple_of(first + i * KEY_BLOCK, KEY_BLOCK), KEY_BLOCK)
        weights.append(weights_of(mul_nt(kv_ref[at, :HD], q), top))
    return weighted(vt_ref, first, weights)


def careful_rows(q_ref, kv_ref, vt_ref, stat_ref, acc_ref, head, count):
    q = q_ref[:, head_cols(head)]

    def block_step(block, carry):
        top, acc = carry
        at = pl.ds(pl.multiple_of(block * KEY_BLOCK, KEY_BLOCK), KEY_BLOCK)
        row = lax.broadcasted_iota(jnp.int32, (KEY_BLOCK, 1), 0) + block * KEY_BLOCK
        scores = jnp.where(row < count, mul_nt(kv_ref[at, :HD], q), -1e30)
        new_top = jnp.maximum(top, jnp.max(scores, axis=0, keepdims=True))
        term = mul(vt_ref[:, at], weights_of(scores, new_top))
        return new_top, acc * jnp.exp2((top - new_top) * EXP2_SCALE) + term

    total = jnp.broadcast_to(stat_ref[1, pl.ds(head, 1), :], (AUG - HD, q.shape[0]))
    acc = jnp.concatenate([acc_ref[head].astype(jnp.float32), total], axis=0)
    return lax.fori_loop(
        0, kv_ref.shape[0] // KEY_BLOCK, block_step, (stat_ref[0, pl.ds(head, 1), :], acc)
    )


def kept_kernel(
    at_ref,
    q_ref,
    mine_ref,
    other_ref,
    stat_a_ref,
    acc_a_ref,
    stat_b_ref,
    acc_b_ref,
    new_stat_ref,
    new_acc_ref,
    stat_ref,
    own_ref,
    sum_ref,
    kv_ref,
    vt_ref,
):
    first = 0
    for stat_part, acc_part in ((stat_a_ref, acc_a_ref), (stat_b_ref, acc_b_ref)):
        heads = acc_part.shape[0]
        stat_ref[:, first : first + heads] = stat_part[...]
        for head in range(heads):
            sum_ref[first + head, :HD] = acc_part[head].astype(jnp.float32)
            total = stat_part[1, head : head + 1, :]
            sum_ref[first + head, HD:] = jnp.broadcast_to(total, (AUG - HD, sum_ref.shape[2]))
        first += heads
    host = at_ref[0]
    chip, core = lax.div(host, 2), lax.rem(host, 2)
    senders, kept_rows, _ = mine_ref.shape
    count = host * kept_rows
    for piece in range(senders):
        y = lax.rem(lax.div(chip, SIDE) + SIDE - piece // SIDE, SIDE)
        x = lax.rem(lax.rem(chip, SIDE) + SIDE - piece % SIDE, SIDE)
        first = (y * SIDE + x) * 2 * kept_rows
        for ref, which in ((mine_ref, core), (other_ref, 1 - core)):
            at = pl.multiple_of(first + which * kept_rows, kept_rows)
            kv_ref[pl.ds(at, kept_rows), :] = ref[piece]
    fill_values(vt_ref, kv_ref)
    spare = lax.broadcasted_iota(jnp.int32, vt_ref.shape, 1) >= count
    vt_ref[...] = jnp.where(spare, 0.0, vt_ref[...]).astype(jnp.bfloat16)
    steps = GROUP // HEAD_STEP

    def step(i, carry):
        first = lax.div(i, steps) * KEPT_BLOCK
        for part in range(HEAD_STEP):
            head = lax.rem(i, steps) * HEAD_STEP + part
            sum_ref[head] += fast_rows(q_ref, kv_ref, vt_ref, stat_ref, head, first, KEPT_BLOCK)
        return carry

    lax.fori_loop(0, lax.div(count + KEPT_BLOCK - 1, KEPT_BLOCK) * steps, step, 0)
    new_stat_ref[0] = stat_ref[0]
    for head in range(GROUP):
        new_acc_ref[head] = sum_ref[head, :HD].astype(jnp.bfloat16)
        new_stat_ref[1, head : head + 1, :] = sum_ref[head, HD : HD + 1]
    safe = jnp.all(new_stat_ref[1] < SAFE_TOTAL)

    @pl.when(jnp.logical_not(safe))
    def careful():
        own_ref[:OWN_FIRST] = acc_a_ref[...]
        own_ref[OWN_FIRST:] = acc_b_ref[...]

        def head_step(head, carry):
            top, acc = careful_rows(q_ref, kv_ref, vt_ref, stat_ref, own_ref, head, count)
            new_stat_ref[0, pl.ds(head, 1), :] = top
            new_stat_ref[1, pl.ds(head, 1), :] = acc[HD : HD + 1]
            new_acc_ref[head] = acc[:HD].astype(jnp.bfloat16)
            return carry

        lax.fori_loop(0, GROUP, head_step, 0)


def anchor_kernel(
    q_ref, kv_ref, stat_ref, acc_ref, out_hbm, out_ref, vt_ref, total_ref, sem
):
    fill_values(vt_ref, kv_ref)
    rows = kv_ref.shape[0]

    def store(head):
        return pltpu.make_async_copy(
            out_ref.at[head], out_hbm.at[:, head_cols(head)], sem.at[head]
        )

    def finish(head, acc, total):
        out_ref[head] = (acc * (1.0 / total)).astype(jnp.bfloat16).T
        store(head).start()

    for head in range(GROUP):
        term = fast_rows(q_ref, kv_ref, vt_ref, stat_ref, head, 0, rows)
        total = stat_ref[1, head : head + 1, :] + term[HD : HD + 1]
        total_ref[head : head + 1, :] = total
        finish(head, acc_ref[head].astype(jnp.float32) + term[:HD], total)
    wait_all([store(head) for head in range(GROUP)])
    safe = jnp.all(total_ref[...] < SAFE_TOTAL)

    @pl.when(jnp.logical_not(safe))
    def careful():
        def head_step(head, carry):
            _, acc = careful_rows(q_ref, kv_ref, vt_ref, stat_ref, acc_ref, head, rows)
            finish(head, acc[:HD], acc[HD : HD + 1])
            store(head).wait()
            return carry

        lax.fori_loop(0, GROUP, head_step, 0)


VMEM = pl.BlockSpec(memory_space=pltpu.VMEM)
SMEM = pl.BlockSpec(memory_space=pltpu.SMEM)


HBM = pl.BlockSpec(memory_space=pltpu.HBM)


def call(kernel, name, in_specs, outs, args, scratch=(), flops=0, nbytes=0, limit=24, out_spec=VMEM):
    return pl.pallas_call(
        kernel,
        in_specs=in_specs,
        out_specs=[out_spec] * len(outs),
        out_shape=[jax.ShapeDtypeStruct(shape, dtype) for shape, dtype in outs],
        scratch_shapes=list(scratch),
        compiler_params=pltpu.CompilerParams(vmem_limit_bytes=limit << 20),
        cost_estimate=pl.CostEstimate(flops=flops, bytes_accessed=nbytes, transcendentals=0),
        name=name,
    )(*args)


def moves(dy, dx, dcore=0):
    pairs = []
    for y in range(SIDE):
        for x in range(SIDE):
            for core in range(2):
                to = ((y + dy) % SIDE * SIDE + (x + dx) % SIDE) * 2 + (core ^ dcore)
                pairs.append(((y * SIDE + x) * 2 + core, to))
    return pairs


def per_device(queries, own_kv, retain, anchor_hidden, w_kv):
    tok, width = own_kv.shape
    hosts = lax.axis_size("hst")
    heads = lax.axis_size("tensor")
    host = lax.axis_index("hst")
    kept_rows = retain.shape[0]
    rows = anchor_hidden.shape[0]
    bf16, f32 = jnp.bfloat16, jnp.float32
    state = [((2, GROUP, tok), f32), ((GROUP, HD, tok), bf16)]
    barrier = lax.optimization_barrier

    dma = pltpu.SemaphoreType.DMA

    def own(first, count, weight, queries, own_kv):
        return call(
            functools.partial(own_kernel, first, count),
            "own",
            [VMEM] * 2,
            [((2, count, tok), f32), ((count, HD, tok), bf16)],
            (queries, own_kv),
            [pltpu.VMEM((AUG, tok), bf16)],
            flops=weight * GROUP * tok * tok * HD,
            nbytes=1 << 10,
        )

    with jax.named_scope("gather_hidden"):
        (hidden,) = call(
            repeat_kernel,
            "repeat",
            [HBM],
            [((heads, *anchor_hidden.shape), bf16)],
            (anchor_hidden,),
            [pltpu.VMEM(anchor_hidden.shape, bf16), dma((2,)), dma((2, heads))],
            nbytes=1 << 20,
            limit=63,
            out_spec=HBM,
        )
        hidden, own_kv, queries, retain = barrier((hidden, own_kv, queries, retain))
        hidden = lax.all_to_all(hidden, "tensor", 0, 0)
    with jax.named_scope("select_kept"):
        (kept,) = call(
            select_kernel,
            "select",
            [HBM] * 2,
            [((kept_rows, width), bf16)],
            (retain.T, own_kv),
            [
                pltpu.VMEM((1, kept_rows), jnp.int32),
                pltpu.VMEM((tok, width), bf16),
                pltpu.VMEM((kept_rows, width), bf16),
                dma((2,)),
            ],
            flops=2 * kept_rows * tok * width,
            nbytes=1 << 18,
            limit=63,
            out_spec=HBM,
        )
        kept, own_kv, queries = barrier((kept, own_kv, queries))
        row = [kept] + [lax.ppermute(kept, "hst", moves(0, d)) for d in range(1, SIDE)]
        own_a = own(0, OWN_FIRST, 0, queries, own_kv)
        *row, stat_a, acc_a = barrier((*row, *own_a))
        row = jnp.stack(row)
        plane = [row] + [lax.ppermute(row, "hst", moves(d, 0)) for d in range(1, SIDE)]
    with jax.named_scope("project"):
        hidden, row = barrier((hidden, row))
        (part,) = call(
            project_kernel,
            "project",
            [VMEM] * 2,
            [((heads * rows, width), bf16)],
            (hidden, w_kv),
            flops=2 * heads * rows * w_kv.shape[0] * width,
            nbytes=5 << 20,
        )
        part = jnp.concatenate([part, lax.ppermute(part, "hst", moves(0, 0, 1))])
        part = jnp.broadcast_to(part[None], (hosts // 2, *part.shape))
        _, own_kv, queries, *plane = barrier((part, own_kv, queries, *plane))
        same_core = [[2 * chip + core for chip in range(hosts // 2)] for core in range(2)]
        anchor = lax.all_to_all(part, "hst", 0, 0, axis_index_groups=same_core)
        anchor = anchor.reshape(hosts * heads * rows, width)
        mine = jnp.concatenate(plane)
        other = lax.ppermute(mine, "hst", moves(0, 0, 1))
    with jax.named_scope("own"):
        stat_b, acc_b = own(OWN_FIRST, GROUP - OWN_FIRST, 320, queries, own_kv)
    with jax.named_scope("kept"):
        stat, acc = call(
            kept_kernel,
            "kept",
            [SMEM] + [VMEM] * 7,
            state,
            (host[None].astype(jnp.int32), queries, mine, other, stat_a, acc_a, stat_b, acc_b),
            [
                *(pltpu.VMEM(*one) for one in state),
                pltpu.VMEM((GROUP, AUG, tok), f32),
                pltpu.VMEM((hosts * kept_rows, width), bf16),
                pltpu.VMEM((AUG, hosts * kept_rows), bf16),
            ],
            flops=4 * GROUP * tok * hosts * kept_rows * HD,
            nbytes=8 << 20,
        )
    with jax.named_scope("anchor"):
        (out,) = call(
            anchor_kernel,
            "anchor",
            [VMEM] * 4,
            [((tok, GROUP * HD), bf16)],
            (queries, anchor, stat, acc),
            [
                pltpu.VMEM((GROUP, tok, HD), bf16),
                pltpu.VMEM((AUG, anchor.shape[0]), bf16),
                pltpu.VMEM((GROUP, tok), f32),
                dma((GROUP,)),
            ],
            out_spec=HBM,
            nbytes=1 << 20,
        )
    return out


def solution(mesh):
    placed = (
        P("hst", "tensor"),
        P("hst", "tensor"),
        P("hst", "tensor"),
        P(("hst", "tensor"), None),
        P(None, "tensor"),
    )
    return jax.shard_map(
        per_device, mesh=mesh, in_specs=placed, out_specs=P("hst", "tensor"), check_vma=False
    )
```
